256 devices in a mesh: fsdp: 32 (over y, x, core), ctx: 8 (over z).
Axes of the slice: x: 4, y: 4, z: 8, core: 2. Of those that a mesh axis runs over, the one named last changes fastest.
Arguments:
- tokens: bfloat16 [16384, 8192], P('fsdp'), may hold values from -12 to 12
- wq: bfloat16 [8192, 4096], P('fsdp', 'ctx'), may hold values from -0.0625 to 0.0625
- wo: bfloat16 [4096, 8192], P('ctx', 'fsdp'), may hold values from -1.5 to 1.5
- key_cache: bfloat16 [65536, 1024], P(('fsdp', 'ctx')), may hold values from -500 to 500, as said below
- value_cache: bfloat16 [65536, 1024], P(('fsdp', 'ctx')), may hold values from -6 to 6
- key_blocks: int32 [32, 4, 8], P('fsdp'), may hold values from 0 to 15, as said below
Outputs:
- mixed: bfloat16 [16384, 8192], P('fsdp', 'ctx')
The draws below stay inside these ranges and needn't reach their ends.
Inputs may be any that keep to these rules, and one draw needn't show every extreme that they name: `key_cache`: keys of order one; a sequence's first block may hold much larger ones. `key_blocks`: for query block b of sequence s, entries 0 to 2 name key blocks 16 - 4 + b - 2, 12 + b - 1 and 12 + b; entries 3 and 4 name blocks 0 and 1; the last 3 entries are random blocks. Counting the random entries of a sequence over its query blocks in order as t = 0, 1, ..., the t-th lies in blocks k * 2 to (k+1) * 2 - 1 with k = 1 + t mod (6); entries may repeat.
All inputs are finite; a program needn't handle non-finite values.
Results may differ from the reference program's by a relative error of at most 0.018.
Values may be sent and summed in bfloat16 or wider, within the bound.
No kernel may reach another device: no remote copies, remote signals or barrier semaphores. Data moves between devices by JAX's collectives and lax.ppermute only.
A program may use at most 128 MiB of HBM per device.

```python
import jax
import jax.numpy as jnp
from jax import lax

D = 8192
HEADS = 32
KV_HEADS = 8
HEAD = 128
BLOCK = 128
QB = 4
RANDS = 3
BLK_DEV = 2
Q_LEN = 512
CACHE_BLOCKS = 16
KEYS = 2048
SEQS = 32
ROWS = 16384
N_CTX = 8


def draw_tokens(key, part):
    base = jnp.clip(jax.random.normal(key, (ROWS, D), jnp.float32), -6.0, 6.0)
    return base.astype(jnp.bfloat16)


def draw_key_cache(key, part):
    width = KV_HEADS * HEAD
    base = jnp.clip(jax.random.normal(key, (SEQS, KEYS, width), jnp.float32), -6.0, 6.0)
    return base.reshape(SEQS * KEYS, width).astype(jnp.bfloat16)


def draw_key_blocks(key, part):
    owner_count = CACHE_BLOCKS // BLK_DEV
    query_ids = jnp.arange(QB, dtype=jnp.int32)
    own_ids = CACHE_BLOCKS - QB + query_ids
    window = own_ids[:, None] + jnp.arange(-2, 1, dtype=jnp.int32)[None, :]
    anchors = jnp.broadcast_to(jnp.arange(2, dtype=jnp.int32)[None, :], (QB, 2))
    entry_ids = jnp.arange(QB * RANDS, dtype=jnp.int32).reshape(QB, RANDS)
    owner_ids = 1 + entry_ids % (owner_count - 2)
    offsets = jax.random.randint(key, (SEQS, QB, RANDS), 0, BLK_DEV, dtype=jnp.int32)
    randoms = owner_ids[None, :, :] * BLK_DEV + offsets
    fixed_part = jnp.concatenate([window, anchors], axis=1)
    listed = jnp.concatenate([jnp.broadcast_to(fixed_part[None, :, :], (SEQS, QB, 5)), randoms], axis=2)
    return listed.astype(jnp.int32)


def levels(stream_key, dims, cuts, least, high):
    def one(position, shards_of):
        draws = jax.random.uniform(jax.random.fold_in(jax.random.fold_in(stream_key, 6), position), (shards_of,), jnp.float32, least / len(cuts), high / len(cuts))
        return jnp.repeat(jnp.exp(draws), dims[position] // shards_of).reshape((-1,) + (1,) * (len(dims) - position - 1))

    gain = one(*cuts[0])
    for cut in cuts[1:]:
        gain = gain * one(*cut)
    return gain


def bell_draw(stream_key, dims, scale, limit, shards=(), held_as=jnp.bfloat16):
    gain = levels(stream_key, dims, shards, -0.22, 0.18) if shards else 1.0
    entries = jax.random.normal(stream_key, dims, jnp.float32) * scale * gain
    return jnp.minimum(jnp.maximum(entries, -limit), limit).astype(held_as)


def setup_inputs(seed: int = 0) -> dict:
    key_list = jax.random.split(jax.random.key(seed), 7)
    return {
        "tokens": draw_tokens(jax.random.fold_in(key_list[6], 71), 0),
        "wq": bell_draw(key_list[1], (D, HEADS * HEAD), D ** -0.5, 0.0625, ((0, 32), (1, 8))),
        "wo": bell_draw(key_list[2], (HEADS * HEAD, D), (HEAD // 8) ** -0.5, 1.5, ((0, 8), (1, 32))),
        "key_cache": draw_key_cache(jax.random.fold_in(key_list[6], 71), 0),
        "value_cache": bell_draw(key_list[4], (SEQS * KEYS, KV_HEADS * HEAD), 1.0, 6.0, ((0, 256),)),
        "key_blocks": draw_key_blocks(jax.random.fold_in(key_list[6], 71), 0),
    }


rope_base = 1000000.0


def rotate(vectors, positions):
    half_width = vectors.shape[-1] // 2
    frequency = rope_base ** (-(jnp.arange(half_width, dtype=jnp.float32) * 2.0) / vectors.shape[-1])
    angles = positions.astype(jnp.float32)[:, None] * frequency[None, :]
    cosine_table = jnp.cos(angles)[:, None, :]
    sine_table = jnp.sin(angles)[:, None, :]
    front_half = vectors[..., :half_width]
    back_half = vectors[..., half_width:]
    return jnp.concatenate([front_half * cosine_table - back_half * sine_table, back_half * cosine_table + front_half * sine_table], axis=-1)


def reference(tokens, wq, wo, key_cache, value_cache, key_blocks):
    group_size = HEADS // KV_HEADS
    positions = (KEYS - Q_LEN) + jnp.arange(Q_LEN, dtype=jnp.int32)
    projected = jnp.dot(tokens, wq, preferred_element_type=jnp.float32).reshape(SEQS, Q_LEN, HEADS, HEAD)
    query = (rotate(projected, positions) * (HEAD ** -0.5)).astype(jnp.bfloat16)
    keys = key_cache.reshape(SEQS, KEYS // BLOCK, BLOCK, KV_HEADS, HEAD)
    values = value_cache.reshape(SEQS, KEYS // BLOCK, BLOCK, KV_HEADS, HEAD)
    own_block = (KEYS - Q_LEN) // BLOCK + jnp.arange(QB, dtype=jnp.int32)
    causal = jnp.arange(BLOCK)[None, :] <= jnp.arange(BLOCK)[:, None]

    def one_sequence(items):
        query_seq, keys_seq, values_seq, lists = items
        picked_keys = jnp.take(keys_seq, lists, axis=0).astype(jnp.float32)
        picked_values = jnp.take(values_seq, lists, axis=0).astype(jnp.float32)
        shaped = query_seq.reshape(QB, BLOCK, KV_HEADS, group_size, HEAD).astype(jnp.float32)
        scores = jnp.einsum("bqkgd,bnskd->bkgqns", shaped, picked_keys)
        own = lists == own_block[:, None]
        allowed = jnp.logical_or(jnp.logical_not(own)[:, None, None, None, :, None], causal[None, None, None, :, None, :])
        scores = jnp.where(allowed, scores, -jnp.inf)
        top_score = jnp.max(scores, axis=(4, 5), keepdims=True)
        raised = jnp.exp(scores - top_score)
        weights = (raised / jnp.sum(raised, axis=(4, 5), keepdims=True)).astype(jnp.bfloat16)
        context = jnp.einsum("bkgqns,bnskd->bqkgd", weights.astype(jnp.float32), picked_values)
        return context.astype(jnp.bfloat16).reshape(Q_LEN, HEADS * HEAD)

    contexts = lax.map(one_sequence, (query, keys, values, key_blocks)).reshape(ROWS, HEADS * HEAD)
    group_cols = (HEADS // N_CTX) * HEAD
    total = jnp.zeros((ROWS, D), jnp.float32)
    for index in range(N_CTX):
        share_sum = jnp.dot(contexts[:, index * group_cols:(index + 1) * group_cols], wo[index * group_cols:(index + 1) * group_cols], preferred_element_type=jnp.float32).astype(jnp.bfloat16)
        share_sum = lax.optimization_barrier(share_sum)
        total = total + share_sum.astype(jnp.float32)
    return total.astype(jnp.bfloat16)
```

```python
import functools

import jax
import jax.numpy as jnp
from jax import lax
from jax.experimental import pallas as pl
from jax.experimental.pallas import tpu as pltpu
from jax.sharding import PartitionSpec as P

HEAD = 128
BLOCK = 128
SIDE = 4
ROPE_BASE = 1000000.0
F32 = jnp.float32
BF16 = jnp.bfloat16
VMEM_LIMIT = 48 * 2**20


def fsdp_index(y, x, core):
    return ((y % SIDE) * SIDE + x % SIDE) * 2 + core


def ring_pairs(phase, step):
    pairs = []
    for y in range(SIDE):
        for x in range(SIDE):
            for core in range(2):
                along_x = (core == 0) == (phase == 0)
                target = (y, x + step) if along_x else (y + step, x)
                pairs.append((fsdp_index(y, x, core), fsdp_index(*target, core)))
    return pairs


CORE_PAIRS = [(f, f ^ 1) for f in range(2 * SIDE * SIDE)]


def swap_cores(block):
    return lax.ppermute(block, "fsdp", CORE_PAIRS)


FIRST = (0, -1, 1, 2)


def block_index(core, first, second):
    me = lax.axis_index("fsdp") // 2
    y, x = me // SIDE, me % SIDE
    dx = jnp.where(core == 0, first, second)
    dy = jnp.where(core == 0, second, first)
    return (((y + dy) % SIDE) * SIDE + (x + dx) % SIDE) * 2 + core


def project_kernel(terms, has_sum, index_ref, *refs):
    tokens, weights = refs[:terms], refs[terms : 2 * terms]
    rest = refs[2 * terms :]
    before = rest[0] if has_sum else None
    out, total = rest[-2], rest[-1]
    step = pl.program_id(0)

    @pl.when(step == 0)
    def _():
        if has_sum:
            total[...] = before[...]
        else:
            total[...] = jnp.zeros_like(total)

    added = jnp.dot(tokens[0][...], weights[0][...], preferred_element_type=F32)
    for t, w in zip(tokens[1:], weights[1:]):
        added += jnp.dot(t[...], w[...], preferred_element_type=F32)
    total[...] += added

    @pl.when(step == pl.num_programs(0) - 1)
    def _():
        out[...] = total[...]


def project(tokens, pieces, index, before=None):
    rows = tokens.shape[0]
    terms = len(pieces)
    depth, cols = tokens.shape[1] // (2 * SIDE * SIDE), pieces[0].shape[1]
    steps = pieces[0].shape[0] // depth

    def token_spec(t):
        return pl.BlockSpec((rows, depth), lambda i, index_ref: (0, index_ref[t, i]))

    whole = pl.BlockSpec((rows, cols), lambda i, index_ref: (0, 0))
    piece_spec = pl.BlockSpec((depth, cols), lambda i, index_ref: (i, 0))
    sums = [] if before is None else [before]
    return pl.pallas_call(
        functools.partial(project_kernel, terms, before is not None),
        grid_spec=pltpu.PrefetchScalarGridSpec(
            num_scalar_prefetch=1,
            grid=(steps,),
            in_specs=[token_spec(t) for t in range(terms)] + [piece_spec] * terms + [whole] * len(sums),
            out_specs=whole,
            scratch_shapes=[pltpu.VMEM((rows, cols), F32)],
        ),
        out_shape=jax.ShapeDtypeStruct((rows, cols), F32),
        compiler_params=pltpu.CompilerParams(vmem_limit_bytes=VMEM_LIMIT),
        cost_estimate=pl.CostEstimate(
            flops=2 * rows * cols * depth * steps * terms,
            bytes_accessed=2 * (rows + cols) * depth * steps * terms + 8 * rows * cols,
            transcendentals=0,
        ),
        name="project",
    )(index, *([tokens] * terms), *pieces, *sums)


def attend_kernel(heads, entries, own_first, blocks_ref, q_ref, cos_ref, sin_ref, kv_ref, out_ref, keys, values):
    b = pl.program_id(0)
    own = own_first + b
    for n in range(entries):
        block = blocks_ref[b, n]
        row = pl.multiple_of((block % 2) * BLOCK, BLOCK)
        keys[pl.ds(n * BLOCK, BLOCK), :] = kv_ref[block // 2, 0, pl.ds(row, BLOCK), :]
        values[pl.ds(n * BLOCK, BLOCK), :] = kv_ref[block // 2, 1, pl.ds(row, BLOCK), :]
    query_row = lax.broadcasted_iota(jnp.int32, (BLOCK, BLOCK), 0)
    key_row = lax.broadcasted_iota(jnp.int32, (BLOCK, BLOCK), 1)
    late = key_row > query_row
    cos, sin = cos_ref[...], sin_ref[...]
    for h in range(heads):
        x = q_ref[:, h * HEAD : (h + 1) * HEAD]
        query = (x * cos + pltpu.roll(x, HEAD // 2, 1) * sin).astype(BF16)
        scores = lax.dot_general(query, keys[...], (((1,), (1,)), ((), ())), preferred_element_type=F32)
        kept = []
        for n in range(entries):
            left_out = jnp.logical_and(late, blocks_ref[b, n] == own)
            kept.append(jnp.where(left_out, -jnp.inf, scores[:, n * BLOCK : (n + 1) * BLOCK]))
        scores = jnp.concatenate(kept, axis=1)
        top = jnp.max(scores, axis=1, keepdims=True)
        raised = jnp.exp(scores - top)
        total = jnp.sum(raised, axis=1, keepdims=True)
        mixed = jnp.dot(raised.astype(BF16), values[...], preferred_element_type=F32)
        out_ref[:, h * HEAD : (h + 1) * HEAD] = (mixed / total).astype(BF16)


def attend(projected, cos, sin, kv, lists):
    rows, cols = projected.shape
    query_blocks, entries = lists.shape
    owners, _, held, _ = kv.shape
    heads = cols // HEAD
    own_first = owners * held // BLOCK - query_blocks
    strip = pl.BlockSpec((BLOCK, cols), lambda b, lists_ref: (b, 0))
    table = pl.BlockSpec((BLOCK, HEAD), lambda b, lists_ref: (b, 0))
    return pl.pallas_call(
        functools.partial(attend_kernel, heads, entries, own_first),
        grid_spec=pltpu.PrefetchScalarGridSpec(
            num_scalar_prefetch=1,
            grid=(query_blocks,),
            in_specs=[strip, table, table, pl.BlockSpec(kv.shape, lambda b, lists_ref: (0, 0, 0, 0))],
            out_specs=strip,
            scratch_shapes=[
                pltpu.VMEM((entries * BLOCK, HEAD), BF16),
                pltpu.VMEM((entries * BLOCK, HEAD), BF16),
            ],
        ),
        out_shape=jax.ShapeDtypeStruct((rows, cols), BF16),
        compiler_params=pltpu.CompilerParams(vmem_limit_bytes=VMEM_LIMIT),
        cost_estimate=pl.CostEstimate(
            flops=4 * rows * entries * BLOCK * cols,
            bytes_accessed=6 * rows * cols + 2 * kv.size,
            transcendentals=rows * heads * entries * BLOCK,
        ),
        name="attend",
    )(lists, projected, cos, sin, kv)


def output_kernel(terms, has_sum, index_ref, *refs):
    contexts, weights = refs[:terms], refs[terms : 2 * terms]
    out = refs[-1]
    total = jnp.dot(contexts[0][...], weights[0][0], preferred_element_type=F32)
    for c, w in zip(contexts[1:], weights[1:]):
        total += jnp.dot(c[...], w[0], preferred_element_type=F32)
    if has_sum:
        total += refs[2 * terms][...]
    out[...] = total.astype(out.dtype)


def output(contexts, weights, index, before=None, dtype=F32):
    rows, depth = contexts[0].shape
    terms = len(contexts)
    blocks, _, width = weights.shape
    owners = 8
    parts = blocks // owners

    def weight_spec(t):
        return pl.BlockSpec((1, depth, width), lambda j, index_ref: (j * owners + index_ref[t], 0, 0))

    strip = pl.BlockSpec((rows, width), lambda j, index_ref: (0, j))
    sums = [] if before is None else [before]
    return pl.pallas_call(
        functools.partial(output_kernel, terms, before is not None),
        grid_spec=pltpu.PrefetchScalarGridSpec(
            num_scalar_prefetch=1,
            grid=(parts,),
            in_specs=[pl.BlockSpec((rows, depth), lambda j, index_ref: (0, 0))] * terms
            + [weight_spec(t) for t in range(terms)]
            + [strip] * len(sums),
            out_specs=strip,
        ),
        out_shape=jax.ShapeDtypeStruct((rows, parts * width), dtype),
        compiler_params=pltpu.CompilerParams(vmem_limit_bytes=VMEM_LIMIT),
        cost_estimate=pl.CostEstimate(
            flops=2 * rows * depth * width * parts * terms,
            bytes_accessed=2 * depth * (rows + width * parts) * terms + 8 * rows * width * parts,
            transcendentals=0,
        ),
        name="output",
    )(index, *contexts, *([weights] * terms), *sums)


def tables(rows, first):
    frequency = ROPE_BASE ** (-(jnp.arange(HEAD // 2, dtype=F32) * 2.0) / HEAD)
    positions = (first + jnp.arange(rows, dtype=jnp.int32)).astype(F32)
    angles = positions[:, None] * frequency[None, :]
    scale = HEAD ** (-0.5)
    cos, sin = jnp.cos(angles) * scale, jnp.sin(angles) * scale
    return jnp.concatenate([cos, cos], axis=1), jnp.concatenate([-sin, sin], axis=1)


def gather_wq(wq):
    minus = lax.ppermute(wq, "fsdp", ring_pairs(0, 1))
    plus = lax.ppermute(wq, "fsdp", ring_pairs(0, -1))
    far = lax.ppermute(wq, "fsdp", ring_pairs(0, 2))
    line = jnp.concatenate([wq, minus, plus, far], axis=0)
    half = line.shape[0] // 2
    line_minus = lax.ppermute(line, "fsdp", ring_pairs(1, 1))
    line_plus = lax.ppermute(line, "fsdp", ring_pairs(1, -1))
    far_top = lax.ppermute(line_minus[:half], "fsdp", ring_pairs(1, 1))
    far_low = lax.ppermute(line_plus[half:], "fsdp", ring_pairs(1, -1))
    groups = [[line], [line_minus, line_plus], [far_top, far_low]]
    return [group + [swap_cores(piece) for piece in group] for group in groups]


def wq_indices():
    core = lax.axis_index("fsdp") % 2
    cores = (core, 1 - core)

    def rows(which, second, firsts):
        return jnp.stack([block_index(which, o, second) for o in firsts])

    return [
        jnp.stack([rows(k, 0, FIRST) for k in cores]),
        jnp.stack([rows(k, s, FIRST) for k in cores for s in (-1, 1)]),
        jnp.stack([rows(k, 2, part) for k in cores for part in (FIRST[:2], FIRST[2:])]),
    ]


def body(tokens, wq, wo, key_cache, value_cache, key_blocks):
    ctx_count = lax.axis_size("ctx")
    fsdp_count = lax.axis_size("fsdp")
    z = lax.axis_index("ctx")
    rows = tokens.shape[0]
    held = key_cache.shape[0]

    groups = gather_wq(wq)

    by_head = jnp.stack(
        [
            key_cache.reshape(held, ctx_count, HEAD).transpose(1, 0, 2),
            value_cache.reshape(held, ctx_count, HEAD).transpose(1, 0, 2),
        ],
        axis=1,
    )
    kv = lax.all_to_all(by_head, "ctx", 0, 0, tiled=True)

    parts = fsdp_count // ctx_count
    moves = []
    for f in range(fsdp_count):
        for c in range(ctx_count):
            plane, part = f // parts, f % parts
            moves.append((f * ctx_count + c, (part * ctx_count + (c + plane) % ctx_count) * ctx_count + plane))
    wo_here = lax.ppermute(wo, ("fsdp", "ctx"), moves)
    weights = lax.all_gather(wo_here, "fsdp", axis=0, tiled=False)

    cos, sin = tables(rows, held * ctx_count - rows)
    projected = None
    for pieces, index in zip(groups, wq_indices()):
        projected = project(tokens, pieces, index, projected)
    context = attend(projected, cos, sin, kv, key_blocks[0])

    def owner(*offsets):
        return jnp.stack([(2 * z + o) % ctx_count for o in offsets])

    right = [(i, (i + 1) % ctx_count) for i in range(ctx_count)]
    left = [(i, (i - 1) % ctx_count) for i in range(ctx_count)]
    half = rows // 2
    down, up = [context], [context]
    for _ in range(3):
        down.append(lax.ppermute(down[-1], "ctx", right))
        up.append(lax.ppermute(up[-1], "ctx", left))
    far_top = lax.ppermute(down[-1][:half], "ctx", right)
    far_low = lax.ppermute(up[-1][half:], "ctx", left)

    total = output([context], weights, owner(0))
    for s in (1, 2, 3):
        total = output([down[s], up[s]], weights, owner(-s, s), total)
    far = jnp.concatenate([far_top, far_low], axis=0)
    return output([far], weights, owner(4), total, BF16)


def solution(mesh):
    in_specs = (
        P("fsdp", None),
        P("fsdp", "ctx"),
        P("ctx", "fsdp"),
        P(("fsdp", "ctx"), None),
        P(("fsdp", "ctx"), None),
        P("fsdp", None, None),
    )
    return jax.shard_map(body, mesh=mesh, in_specs=in_specs, out_specs=P("fsdp", "ctx"), check_vma=False)
```

```python
import functools

import jax
import jax.numpy as jnp
from jax import lax
from jax.experimental import pallas as pl
from jax.experimental.pallas import tpu as pltpu
from jax.sharding import PartitionSpec as P

HEAD = 128
BLOCK = 128
SIDE = 4
ROPE_BASE = 1000000.0
F32 = jnp.float32
BF16 = jnp.bfloat16
VMEM_LIMIT = 48 * 2**20


def fsdp_index(y, x, core):
    return ((y % SIDE) * SIDE + x % SIDE) * 2 + core


def ring_pairs(phase, step):
    pairs = []
    for y in range(SIDE):
        for x in range(SIDE):
            for core in range(2):
                along_x = (core == 0) == (phase == 0)
                target = (y, x + step) if along_x else (y + step, x)
                pairs.append((fsdp_index(y, x, core), fsdp_index(*target, core)))
    return pairs


CORE_PAIRS = [(f, f ^ 1) for f in range(2 * SIDE * SIDE)]


def swap_cores(block):
    return lax.ppermute(block, "fsdp", CORE_PAIRS)


FIRST = (0, -1, 1, 2)


def block_index(core, first, second):
    me = lax.axis_index("fsdp") // 2
    y, x = me // SIDE, me % SIDE
    dx = jnp.where(core == 0, first, second)
    dy = jnp.where(core == 0, second, first)
    return (((y + dy) % SIDE) * SIDE + (x + dx) % SIDE) * 2 + core


def project_kernel(terms, has_sum, index_ref, *refs):
    tokens, weights = refs[:terms], refs[terms : 2 * terms]
    rest = refs[2 * terms :]
    before = rest[0] if has_sum else None
    out, total = rest[-2], rest[-1]
    step = pl.program_id(0)

    @pl.when(step == 0)
    def _():
        if has_sum:
            total[...] = before[...]
        else:
            total[...] = jnp.zeros_like(total)

    added = jnp.dot(tokens[0][...], weights[0][...], preferred_element_type=F32)
    for t, w in zip(tokens[1:], weights[1:]):
        added += jnp.dot(t[...], w[...], preferred_element_type=F32)
    total[...] += added

    @pl.when(step == pl.num_programs(0) - 1)
    def _():
        out[...] = total[...]


def project(tokens, pieces, index, before=None):
    rows = tokens.shape[0]
    terms = len(pieces)
    depth, cols = tokens.shape[1] // (2 * SIDE * SIDE), pieces[0].shape[1]
    steps = pieces[0].shape[0] // depth

    def token_spec(t):
        return pl.BlockSpec((rows, depth), lambda i, index_ref: (0, index_ref[t, i]))

    whole = pl.BlockSpec((rows, cols), lambda i, index_ref: (0, 0))
    piece_spec = pl.BlockSpec((depth, cols), lambda i, index_ref: (i, 0))
    sums = [] if before is None else [before]
    return pl.pallas_call(
        functools.partial(project_kernel, terms, before is not None),
        grid_spec=pltpu.PrefetchScalarGridSpec(
            num_scalar_prefetch=1,
            grid=(steps,),
            in_specs=[token_spec(t) for t in range(terms)] + [piece_spec] * terms + [whole] * len(sums),
            out_specs=whole,
            scratch_shapes=[pltpu.VMEM((rows, cols), F32)],
        ),
        out_shape=jax.ShapeDtypeStruct((rows, cols), F32),
        compiler_params=pltpu.CompilerParams(vmem_limit_bytes=VMEM_LIMIT),
        cost_estimate=pl.CostEstimate(
            flops=2 * rows * cols * depth * steps * terms,
            bytes_accessed=2 * (rows + cols) * depth * steps * terms + 8 * rows * cols,
            transcendentals=0,
        ),
        name="project",
    )(index, *([tokens] * terms), *pieces, *sums)


def attend_kernel(heads, entries, first, own_first, blocks_ref, q_ref, cos_ref, sin_ref, kv_ref, out_ref, keys, values, queries):
    b = first + pl.program_id(0)
    own = own_first + b
    for n in range(entries):
        block = blocks_ref[b, n]
        row = pl.multiple_of((block % 2) * BLOCK, BLOCK)
        keys[pl.ds(n * BLOCK, BLOCK), :] = kv_ref[block // 2, 0, pl.ds(row, BLOCK), :]
        values[pl.ds(n * BLOCK, BLOCK), :] = kv_ref[block // 2, 1, pl.ds(row, BLOCK), :]
    query_row = lax.broadcasted_iota(jnp.int32, (BLOCK, BLOCK), 0)
    key_row = lax.broadcasted_iota(jnp.int32, (BLOCK, BLOCK), 1)
    late = key_row > query_row
    cos, sin = cos_ref[...], sin_ref[...]
    for h in range(heads):
        x = q_ref[:, h * HEAD : (h + 1) * HEAD]
        queries[h * BLOCK : (h + 1) * BLOCK, :] = (x * cos + pltpu.roll(x, HEAD // 2, 1) * sin).astype(BF16)
    scores = lax.dot_general(queries[...], keys[...], (((1,), (1,)), ((), ())), preferred_element_type=F32)
    hidden = [jnp.logical_and(late, blocks_ref[b, n] == own) for n in range(entries)]
    for h in range(heads):
        strip = scores[h * BLOCK : (h + 1) * BLOCK, :]
        kept = [jnp.where(hidden[n], -jnp.inf, strip[:, n * BLOCK : (n + 1) * BLOCK]) for n in range(entries)]
        strip = jnp.concatenate(kept, axis=1)
        raised = jnp.exp(strip - jnp.max(strip, axis=1, keepdims=True))
        total = jnp.sum(raised, axis=1, keepdims=True)
        mixed = jnp.dot(raised.astype(BF16), values[...], preferred_element_type=F32)
        out_ref[:, h * HEAD : (h + 1) * HEAD] = (mixed / total).astype(BF16)


def attend(projected, cos, sin, kv, lists, first, count):
    cols = projected.shape[1]
    query_blocks, entries = lists.shape
    owners, _, held, _ = kv.shape
    heads = cols // HEAD
    rows = count * BLOCK
    own_first = owners * held // BLOCK - query_blocks
    table = pl.BlockSpec((BLOCK, HEAD), lambda b, lists_ref: (first + b, 0))
    return pl.pallas_call(
        functools.partial(attend_kernel, heads, entries, first, own_first),
        grid_spec=pltpu.PrefetchScalarGridSpec(
            num_scalar_prefetch=1,
            grid=(count,),
            in_specs=[
                pl.BlockSpec((BLOCK, cols), lambda b, lists_ref: (first + b, 0)),
                table,
                table,
                pl.BlockSpec(kv.shape, lambda b, lists_ref: (0, 0, 0, 0)),
            ],
            out_specs=pl.BlockSpec((BLOCK, cols), lambda b, lists_ref: (b, 0)),
            scratch_shapes=[
                pltpu.VMEM((entries * BLOCK, HEAD), BF16),
                pltpu.VMEM((entries * BLOCK, HEAD), BF16),
                pltpu.VMEM((heads * BLOCK, HEAD), BF16),
            ],
        ),
        out_shape=jax.ShapeDtypeStruct((rows, cols), BF16),
        compiler_params=pltpu.CompilerParams(vmem_limit_bytes=VMEM_LIMIT),
        cost_estimate=pl.CostEstimate(
            flops=4 * rows * entries * BLOCK * cols,
            bytes_accessed=6 * rows * cols + 2 * kv.size,
            transcendentals=rows * heads * entries * BLOCK,
        ),
        name="attend",
    )(lists, projected, cos, sin, kv)


def output_kernel(terms, has_sum, index_ref, *refs):
    contexts, weights = refs[: 2 * terms], refs[2 * terms : 3 * terms]
    out = refs[-1]
    rows = contexts[0].shape[0]
    for half in range(2):
        here = pl.ds(half * rows, rows)
        total = jnp.dot(contexts[half][...], weights[0][0], preferred_element_type=F32)
        for t in range(1, terms):
            total += jnp.dot(contexts[2 * t + half][...], weights[t][0], preferred_element_type=F32)
        if has_sum:
            total += refs[3 * terms][here, :]
        out[here, :] = total.astype(out.dtype)


def output(contexts, weights, index, before=None, dtype=F32):
    rows, depth = contexts[0][0].shape
    terms = len(contexts)
    width = weights.shape[2]
    parts = index.shape[1]

    def weight_spec(t):
        return pl.BlockSpec((1, depth, width), lambda j, index_ref: (index_ref[t, j], 0, 0))

    strip = pl.BlockSpec((2 * rows, width), lambda j, index_ref: (0, j))
    sums = [] if before is None else [before]
    return pl.pallas_call(
        functools.partial(output_kernel, terms, before is not None),
        grid_spec=pltpu.PrefetchScalarGridSpec(
            num_scalar_prefetch=1,
            grid=(parts,),
            in_specs=[pl.BlockSpec((rows, depth), lambda j, index_ref: (0, 0))] * (2 * terms)
            + [weight_spec(t) for t in range(terms)]
            + [strip] * len(sums),
            out_specs=strip,
        ),
        out_shape=jax.ShapeDtypeStruct((2 * rows, parts * width), dtype),
        compiler_params=pltpu.CompilerParams(vmem_limit_bytes=VMEM_LIMIT),
        cost_estimate=pl.CostEstimate(
            flops=4 * rows * depth * width * parts * terms,
            bytes_accessed=2 * depth * (2 * rows + width * parts) * terms + 16 * rows * width * parts,
            transcendentals=0,
        ),
        name="output",
    )(index, *[c for pair in contexts for c in pair], *([weights] * terms), *sums)


def tables(rows, first):
    frequency = ROPE_BASE ** (-(jnp.arange(HEAD // 2, dtype=F32) * 2.0) / HEAD)
    positions = (first + jnp.arange(rows, dtype=jnp.int32)).astype(F32)
    angles = positions[:, None] * frequency[None, :]
    scale = HEAD ** (-0.5)
    cos, sin = jnp.cos(angles) * scale, jnp.sin(angles) * scale
    return jnp.concatenate([cos, cos], axis=1), jnp.concatenate([-sin, sin], axis=1)


def side_by_side_kernel(count, *refs):
    pieces, out, done = refs[:count], refs[count], refs[count + 1]
    copies = []
    start = 0
    for n, piece in enumerate(pieces):
        size = piece.shape[0]
        copies.append(pltpu.make_async_copy(piece, out.at[pl.ds(start, size)], done.at[n]))
        start += size
    for copy in copies:
        copy.start()
    for copy in copies:
        copy.wait()


def side_by_side(pieces):
    total = sum(p.shape[0] for p in pieces)
    anywhere = pl.BlockSpec(memory_space=pl.ANY)
    out = jax.ShapeDtypeStruct((total,) + pieces[0].shape[1:], pieces[0].dtype)
    return pl.pallas_call(
        functools.partial(side_by_side_kernel, len(pieces)),
        in_specs=[anywhere] * len(pieces),
        out_specs=anywhere,
        out_shape=out,
        scratch_shapes=[pltpu.SemaphoreType.DMA((len(pieces),))],
        compiler_params=pltpu.CompilerParams(vmem_limit_bytes=VMEM_LIMIT),
        cost_estimate=pl.CostEstimate(flops=0, bytes_accessed=4 * out.size, transcendentals=0),
        name="side_by_side",
    )(*pieces)


def split_heads_kernel(keys, values, out):
    out[0, 0] = keys[...]
    out[0, 1] = values[...]


def split_heads(keys, values):
    held, cols = keys.shape
    heads = cols // HEAD
    column = pl.BlockSpec((held, HEAD), lambda h: (0, h))
    return pl.pallas_call(
        split_heads_kernel,
        grid=(heads,),
        in_specs=[column, column],
        out_specs=pl.BlockSpec((1, 2, held, HEAD), lambda h: (h, 0, 0, 0)),
        out_shape=jax.ShapeDtypeStruct((heads, 2, held, HEAD), keys.dtype),
        compiler_params=pltpu.CompilerParams(vmem_limit_bytes=VMEM_LIMIT),
        cost_estimate=pl.CostEstimate(flops=0, bytes_accessed=8 * keys.size, transcendentals=0),
        name="split_heads",
    )(keys, values)


def after(value, *earlier):
    return lax.optimization_barrier((value,) + earlier)[0]


def wo_target(f, c):
    core, x, y = f % 2, f // 2 % SIDE, f // 2 // SIDE
    x_to = jnp.where(c % 2 == 0, x, x + jnp.where(x % 2 == 0, -1, 1))
    return fsdp_index(y + c // 2, x_to, core)


def wo_moves(fsdp_count, ctx_count):
    parts = fsdp_count // ctx_count
    moves = []
    for f in range(fsdp_count):
        for c in range(ctx_count):
            core, x, y = f % 2, f // 2 % SIDE, f // 2 // SIDE
            x_to = x if c % 2 == 0 else x + (-1 if x % 2 == 0 else 1)
            moves.append((f * ctx_count + c, fsdp_index(y + c // 2, x_to, core) * ctx_count + f // parts))
    return moves


def project_all(tokens, wq, by_head):
    own_line, near, far_away = wq_indices()
    minus = lax.ppermute(wq, "fsdp", ring_pairs(0, 1))
    plus = lax.ppermute(wq, "fsdp", ring_pairs(0, -1))
    far = lax.ppermute(wq, "fsdp", ring_pairs(0, 2))
    line = side_by_side([wq, minus, plus, after(far, by_head)])
    kv = lax.all_to_all(after(by_head, line), "ctx", 0, 0, tiled=True)
    half = line.shape[0] // 2
    line_minus = lax.ppermute(line, "fsdp", ring_pairs(1, 1))
    line_plus = lax.ppermute(line, "fsdp", ring_pairs(1, -1))
    first = project(tokens, [line, swap_cores(line)], own_line)
    top, low, waited = lax.optimization_barrier((line_minus[:half], line_plus[half:], first))
    far_top = lax.ppermute(top, "fsdp", ring_pairs(1, 1))
    far_low = lax.ppermute(low, "fsdp", ring_pairs(1, -1))
    second = project(
        tokens, [line_minus, line_plus, swap_cores(line_minus), swap_cores(line_plus)], near, waited
    )
    far_top, far_low, second, kv = lax.optimization_barrier((far_top, far_low, second, kv))
    third = project(tokens, [far_top, far_low, swap_cores(far_top), swap_cores(far_low)], far_away, second)
    return third, kv, second


def wq_indices():
    core = lax.axis_index("fsdp") % 2
    cores = (core, 1 - core)

    def rows(which, second, firsts):
        return jnp.stack([block_index(which, o, second) for o in firsts])

    return [
        jnp.stack([rows(k, 0, FIRST) for k in cores]),
        jnp.stack([rows(k, s, FIRST) for k in cores for s in (-1, 1)]),
        jnp.stack([rows(k, 2, part) for k in cores for part in (FIRST[:2], FIRST[2:])]),
    ]


def body(tokens, wq, wo, key_cache, value_cache, key_blocks):
    ctx_count = lax.axis_size("ctx")
    fsdp_count = lax.axis_size("fsdp")
    z = lax.axis_index("ctx")
    rows = tokens.shape[0]
    held = key_cache.shape[0]

    parts = fsdp_count // ctx_count
    wo_here = lax.ppermute(wo, ("fsdp", "ctx"), wo_moves(fsdp_count, ctx_count))
    by_head = split_heads(key_cache, value_cache)
    projected, kv, begun = project_all(tokens, wq, by_head)
    weights = lax.all_gather(after(wo_here, begun), "fsdp", axis=0, tiled=False)

    cos, sin = tables(rows, held * ctx_count - rows)
    blocks = rows // BLOCK // 2
    contexts = [attend(projected, cos, sin, kv, key_blocks[0], n * blocks, blocks) for n in range(2)]

    def owner(*offsets):
        def at(offset):
            return jnp.stack([wo_target(z * parts + j, (z + offset) % ctx_count) for j in range(parts)])

        return jnp.stack([at(o) for o in offsets])

    right = [(i, (i + 1) % ctx_count) for i in range(ctx_count)]
    left = [(i, (i - 1) % ctx_count) for i in range(ctx_count)]
    down, up = [contexts], [contexts]
    for _ in range(3):
        down.append([lax.ppermute(c, "ctx", right) for c in down[-1]])
        up.append([lax.ppermute(c, "ctx", left) for c in up[-1]])
    weights, last_down, last_up = lax.optimization_barrier((weights, down[3][0], up[3][1]))
    far = [lax.ppermute(last_down, "ctx", right), lax.ppermute(last_up, "ctx", left)]

    total = output([contexts, down[1], up[1], down[2], up[2]], weights, owner(0, -1, 1, -2, 2))
    return output([down[3], up[3], far], weights, owner(-3, 3, 4), total, BF16)


def solution(mesh):
    in_specs = (
        P("fsdp", None),
        P("fsdp", "ctx"),
        P("ctx", "fsdp"),
        P(("fsdp", "ctx"), None),
        P(("fsdp", "ctx"), None),
        P("fsdp", None, None),
    )
    return jax.shard_map(body, mesh=mesh, in_specs=in_specs, out_specs=P("fsdp", "ctx"), check_vma=False)
```

```python
import functools

import jax
import jax.numpy as jnp
from jax import lax
from jax.experimental import pallas as pl
from jax.experimental.pallas import tpu as pltpu
from jax.sharding import PartitionSpec as P

HEAD = 128
BLOCK = 128
SIDE = 4
ROPE_BASE = 1000000.0
F32 = jnp.float32
BF16 = jnp.bfloat16
VMEM_LIMIT = 48 * 2**20


def fsdp_index(y, x, core):
    return ((y % SIDE) * SIDE + x % SIDE) * 2 + core


def ring_pairs(phase, step):
    pairs = []
    for y in range(SIDE):
        for x in range(SIDE):
            for core in range(2):
                along_x = (core == 0) == (phase == 0)
                target = (y, x + step) if along_x else (y + step, x)
                pairs.append((fsdp_index(y, x, core), fsdp_index(*target, core)))
    return pairs


CORE_PAIRS = [(f, f ^ 1) for f in range(2 * SIDE * SIDE)]


def swap_cores(block):
    return lax.ppermute(block, "fsdp", CORE_PAIRS)


FIRST = (0, -1, 1, 2)


def block_index(core, first, second):
    me = lax.axis_index("fsdp") // 2
    y, x = me // SIDE, me % SIDE
    dx = jnp.where(core == 0, first, second)
    dy = jnp.where(core == 0, second, first)
    return (((y + dy) % SIDE) * SIDE + (x + dx) % SIDE) * 2 + core


def project_kernel(terms, has_sum, index_ref, *refs):
    tokens, weights = refs[:terms], refs[terms : 2 * terms]
    rest = refs[2 * terms :]
    before = rest[0] if has_sum else None
    out, total = rest[-2], rest[-1]
    step = pl.program_id(0)

    @pl.when(step == 0)
    def _():
        if has_sum:
            total[...] = before[...]
        else:
            total[...] = jnp.zeros_like(total)

    added = jnp.dot(tokens[0][...], weights[0][...], preferred_element_type=F32)
    for t, w in zip(tokens[1:], weights[1:]):
        added += jnp.dot(t[...], w[...], preferred_element_type=F32)
    total[...] += added

    @pl.when(step == pl.num_programs(0) - 1)
    def _():
        out[...] = total[...]


def project(tokens, pieces, index, before=None):
    rows = tokens.shape[0]
    terms = len(pieces)
    depth, cols = tokens.shape[1] // (2 * SIDE * SIDE), pieces[0].shape[1]
    steps = pieces[0].shape[0] // depth

    def token_spec(t):
        return pl.BlockSpec((rows, depth), lambda i, index_ref: (0, index_ref[t, i]))

    whole = pl.BlockSpec((rows, cols), lambda i, index_ref: (0, 0))
    piece_spec = pl.BlockSpec((depth, cols), lambda i, index_ref: (i, 0))
    sums = [] if before is None else [before]
    return pl.pallas_call(
        functools.partial(project_kernel, terms, before is not None),
        grid_spec=pltpu.PrefetchScalarGridSpec(
            num_scalar_prefetch=1,
            grid=(steps,),
            in_specs=[token_spec(t) for t in range(terms)] + [piece_spec] * terms + [whole] * len(sums),
            out_specs=whole,
            scratch_shapes=[pltpu.VMEM((rows, cols), F32)],
        ),
        out_shape=jax.ShapeDtypeStruct((rows, cols), F32),
        compiler_params=pltpu.CompilerParams(vmem_limit_bytes=VMEM_LIMIT),
        cost_estimate=pl.CostEstimate(
            flops=2 * rows * cols * depth * steps * terms,
            bytes_accessed=2 * (rows + cols) * depth * steps * terms + 8 * rows * cols,
            transcendentals=0,
        ),
        name="project",
    )(index, *([tokens] * terms), *pieces, *sums)


def attend_kernel(heads, entries, first, own_first, blocks_ref, q_ref, cos_ref, sin_ref, kv_ref, out_ref, keys, values, queries):
    b = first + pl.program_id(0)
    own = own_first + b
    for n in range(entries):
        block = blocks_ref[b, n]
        row = pl.multiple_of((block % 2) * BLOCK, BLOCK)
        keys[pl.ds(n * BLOCK, BLOCK), :] = kv_ref[block // 2, 0, pl.ds(row, BLOCK), :]
        values[pl.ds(n * BLOCK, BLOCK), :] = kv_ref[block // 2, 1, pl.ds(row, BLOCK), :]
    query_row = lax.broadcasted_iota(jnp.int32, (BLOCK, BLOCK), 0)
    key_row = lax.broadcasted_iota(jnp.int32, (BLOCK, BLOCK), 1)
    late = key_row > query_row
    cos, sin = cos_ref[...], sin_ref[...]
    for h in range(heads):
        x = q_ref[:, h * HEAD : (h + 1) * HEAD]
        queries[h * BLOCK : (h + 1) * BLOCK, :] = (x * cos + pltpu.roll(x, HEAD // 2, 1) * sin).astype(BF16)
    scores = lax.dot_general(queries[...], keys[...], (((1,), (1,)), ((), ())), preferred_element_type=F32)
    hidden = [jnp.logical_and(late, blocks_ref[b, n] == own) for n in range(entries)]
    for h in range(heads):
        strip = scores[h * BLOCK : (h + 1) * BLOCK, :]
        kept = [jnp.where(hidden[n], -jnp.inf, strip[:, n * BLOCK : (n + 1) * BLOCK]) for n in range(entries)]
        strip = jnp.concatenate(kept, axis=1)
        raised = jnp.exp(strip - jnp.max(strip, axis=1, keepdims=True))
        total = jnp.sum(raised, axis=1, keepdims=True)
        mixed = jnp.dot(raised.astype(BF16), values[...], preferred_element_type=F32)
        out_ref[:, h * HEAD : (h + 1) * HEAD] = (mixed / total).astype(BF16)


def attend(projected, cos, sin, kv, lists, first, count):
    cols = projected.shape[1]
    query_blocks, entries = lists.shape
    owners, _, held, _ = kv.shape
    heads = cols // HEAD
    rows = count * BLOCK
    own_first = owners * held // BLOCK - query_blocks
    table = pl.BlockSpec((BLOCK, HEAD), lambda b, lists_ref: (first + b, 0))
    return pl.pallas_call(
        functools.partial(attend_kernel, heads, entries, first, own_first),
        grid_spec=pltpu.PrefetchScalarGridSpec(
            num_scalar_prefetch=1,
            grid=(count,),
            in_specs=[
                pl.BlockSpec((BLOCK, cols), lambda b, lists_ref: (first + b, 0)),
                table,
                table,
                pl.BlockSpec(kv.shape, lambda b, lists_ref: (0, 0, 0, 0)),
            ],
            out_specs=pl.BlockSpec((BLOCK, cols), lambda b, lists_ref: (b, 0)),
            scratch_shapes=[
                pltpu.VMEM((entries * BLOCK, HEAD), BF16),
                pltpu.VMEM((entries * BLOCK, HEAD), BF16),
                pltpu.VMEM((heads * BLOCK, HEAD), BF16),
            ],
        ),
        out_shape=jax.ShapeDtypeStruct((rows, cols), BF16),
        compiler_params=pltpu.CompilerParams(vmem_limit_bytes=VMEM_LIMIT),
        cost_estimate=pl.CostEstimate(
            flops=4 * rows * entries * BLOCK * cols,
            bytes_accessed=6 * rows * cols + 2 * kv.size,
            transcendentals=rows * heads * entries * BLOCK,
        ),
        name="attend",
    )(lists, projected, cos, sin, kv)


def output_kernel(terms, has_sum, index_ref, *refs):
    contexts, weights = refs[: 2 * terms], refs[2 * terms : 3 * terms]
    out = refs[-1]
    rows = contexts[0].shape[0]
    for half in range(2):
        here = pl.ds(half * rows, rows)
        total = jnp.dot(contexts[half][...], weights[0][0], preferred_element_type=F32)
        for t in range(1, terms):
            total += jnp.dot(contexts[2 * t + half][...], weights[t][0], preferred_element_type=F32)
        if has_sum:
            total += refs[3 * terms][here, :]
        out[here, :] = total.astype(out.dtype)


def output(contexts, weights, index, before=None, dtype=F32):
    rows, depth = contexts[0][0].shape
    terms = len(contexts)
    width = weights.shape[2]
    parts = index.shape[1]

    def weight_spec(t):
        return pl.BlockSpec((1, depth, width), lambda j, index_ref: (index_ref[t, j], 0, 0))

    strip = pl.BlockSpec((2 * rows, width), lambda j, index_ref: (0, j))
    sums = [] if before is None else [before]
    return pl.pallas_call(
        functools.partial(output_kernel, terms, before is not None),
        grid_spec=pltpu.PrefetchScalarGridSpec(
            num_scalar_prefetch=1,
            grid=(parts,),
            in_specs=[pl.BlockSpec((rows, depth), lambda j, index_ref: (0, 0))] * (2 * terms)
            + [weight_spec(t) for t in range(terms)]
            + [strip] * len(sums),
            out_specs=strip,
        ),
        out_shape=jax.ShapeDtypeStruct((2 * rows, parts * width), dtype),
        compiler_params=pltpu.CompilerParams(vmem_limit_bytes=VMEM_LIMIT),
        cost_estimate=pl.CostEstimate(
            flops=4 * rows * depth * width * parts * terms,
            bytes_accessed=2 * depth * (2 * rows + width * parts) * terms + 16 * rows * width * parts,
            transcendentals=0,
        ),
        name="output",
    )(index, *[c for pair in contexts for c in pair], *([weights] * terms), *sums)


def tables(rows, first):
    frequency = ROPE_BASE ** (-(jnp.arange(HEAD // 2, dtype=F32) * 2.0) / HEAD)
    positions = (first + jnp.arange(rows, dtype=jnp.int32)).astype(F32)
    angles = positions[:, None] * frequency[None, :]
    scale = HEAD ** (-0.5)
    cos, sin = jnp.cos(angles) * scale, jnp.sin(angles) * scale
    return jnp.concatenate([cos, cos], axis=1), jnp.concatenate([-sin, sin], axis=1)


def side_by_side_kernel(count, *refs):
    pieces, out, done = refs[:count], refs[count], refs[count + 1]
    copies = []
    start = 0
    for n, piece in enumerate(pieces):
        size = piece.shape[0]
        copies.append(pltpu.make_async_copy(piece, out.at[pl.ds(start, size)], done.at[n]))
        start += size
    for copy in copies:
        copy.start()
    for copy in copies:
        copy.wait()


def side_by_side(pieces):
    total = sum(p.shape[0] for p in pieces)
    anywhere = pl.BlockSpec(memory_space=pl.ANY)
    out = jax.ShapeDtypeStruct((total,) + pieces[0].shape[1:], pieces[0].dtype)
    return pl.pallas_call(
        functools.partial(side_by_side_kernel, len(pieces)),
        in_specs=[anywhere] * len(pieces),
        out_specs=anywhere,
        out_shape=out,
        scratch_shapes=[pltpu.SemaphoreType.DMA((len(pieces),))],
        compiler_params=pltpu.CompilerParams(vmem_limit_bytes=VMEM_LIMIT),
        cost_estimate=pl.CostEstimate(flops=0, bytes_accessed=4 * out.size, transcendentals=0),
        name="side_by_side",
    )(*pieces)


def split_heads_kernel(keys, values, out):
    out[0, 0] = keys[...]
    out[0, 1] = values[...]


def split_heads(keys, values):
    held, cols = keys.shape
    heads = cols // HEAD
    column = pl.BlockSpec((held, HEAD), lambda h: (0, h))
    return pl.pallas_call(
        split_heads_kernel,
        grid=(heads,),
        in_specs=[column, column],
        out_specs=pl.BlockSpec((1, 2, held, HEAD), lambda h: (h, 0, 0, 0)),
        out_shape=jax.ShapeDtypeStruct((heads, 2, held, HEAD), keys.dtype),
        compiler_params=pltpu.CompilerParams(vmem_limit_bytes=VMEM_LIMIT),
        cost_estimate=pl.CostEstimate(flops=0, bytes_accessed=8 * keys.size, transcendentals=0),
        name="split_heads",
    )(keys, values)


def after(value, *earlier):
    return lax.optimization_barrier((value,) + earlier)[0]


def wo_target(f, c):
    core, x, y = f % 2, f // 2 % SIDE, f // 2 // SIDE
    x_to = jnp.where(c % 2 == 0, x, x + jnp.where(x % 2 == 0, -1, 1))
    return fsdp_index(y + c // 2, x_to, core)


def wo_moves(fsdp_count, ctx_count):
    parts = fsdp_count // ctx_count
    within, across = [], []
    for f in range(fsdp_count):
        for c in range(ctx_count):
            core, x, y = f % 2, f // 2 % SIDE, f // 2 // SIDE
            x_to = x if c % 2 == 0 else x + (-1 if x % 2 == 0 else 1)
            target = fsdp_index(y + c // 2, x_to, core) * ctx_count
            within.append((f * ctx_count + c, target + c))
            across.append((target + c, target + f // parts))
    return within, across


def project_all(tokens, wq, by_head, wo_near, wo_across, turns):
    own_line, near, far_away = wq_indices()
    minus = lax.ppermute(wq, "fsdp", ring_pairs(0, 1))
    plus = lax.ppermute(wq, "fsdp", ring_pairs(0, -1))
    far = lax.ppermute(wq, "fsdp", ring_pairs(0, 2))
    far, _, wo_near, turns = lax.optimization_barrier((far, by_head, wo_near, turns))
    line = side_by_side([wq, minus, plus, far])
    wo_here = lax.ppermute(wo_near, ("fsdp", "ctx"), wo_across)
    kv = lax.all_to_all(after(by_head, wo_here), "ctx", 0, 0, tiled=True)
    half = line.shape[0] // 2
    line_minus = lax.ppermute(line, "fsdp", ring_pairs(1, 1))
    line_plus = lax.ppermute(line, "fsdp", ring_pairs(1, -1))
    first = project(tokens, [line, swap_cores(line)], own_line)
    top, low, waited = lax.optimization_barrier((line_minus[:half], line_plus[half:], first))
    far_top = lax.ppermute(top, "fsdp", ring_pairs(1, 1))
    far_low = lax.ppermute(low, "fsdp", ring_pairs(1, -1))
    second = project(
        tokens, [line_minus, line_plus, swap_cores(line_minus), swap_cores(line_plus)], near, waited
    )
    far_top, far_low, second = lax.optimization_barrier((far_top, far_low, second))
    third = project(tokens, [far_top, far_low, swap_cores(far_top), swap_cores(far_low)], far_away, second)
    return third, turns, kv, after(wo_here, first, line_minus, line_plus)


def wq_indices():
    core = lax.axis_index("fsdp") % 2
    cores = (core, 1 - core)

    def rows(which, second, firsts):
        return jnp.stack([block_index(which, o, second) for o in firsts])

    return [
        jnp.stack([rows(k, 0, FIRST) for k in cores]),
        jnp.stack([rows(k, s, FIRST) for k in cores for s in (-1, 1)]),
        jnp.stack([rows(k, 2, part) for k in cores for part in (FIRST[:2], FIRST[2:])]),
    ]


def body(tokens, wq, wo, key_cache, value_cache, key_blocks):
    ctx_count = lax.axis_size("ctx")
    fsdp_count = lax.axis_size("fsdp")
    z = lax.axis_index("ctx")
    rows = tokens.shape[0]
    held = key_cache.shape[0]

    parts = fsdp_count // ctx_count
    within, across = wo_moves(fsdp_count, ctx_count)
    wo_near = lax.ppermute(wo, ("fsdp", "ctx"), within)
    by_head = split_heads(key_cache, value_cache)
    turns = tables(rows, held * ctx_count - rows)
    projected, (cos, sin), kv, wo_here = project_all(tokens, wq, by_head, wo_near, across, turns)
    weights = lax.all_gather(wo_here, "fsdp", axis=0, tiled=False)

    blocks = rows // BLOCK // 2
    contexts = [attend(projected, cos, sin, kv, key_blocks[0], n * blocks, blocks) for n in range(2)]

    def owner(*offsets):
        def at(offset):
            return jnp.stack([wo_target(z * parts + j, (z + offset) % ctx_count) for j in range(parts)])

        return jnp.stack([at(o) for o in offsets])

    right = [(i, (i + 1) % ctx_count) for i in range(ctx_count)]
    left = [(i, (i - 1) % ctx_count) for i in range(ctx_count)]
    down, up = [contexts], [contexts]
    for _ in range(3):
        down.append([lax.ppermute(c, "ctx", right) for c in down[-1]])
        up.append([lax.ppermute(c, "ctx", left) for c in up[-1]])
    far = [lax.ppermute(down[3][0], "ctx", right), lax.ppermute(up[3][1], "ctx", left)]
    near = [contexts, down[1], up[1], down[2], up[2], down[3], up[3]]
    return output(near + [far], weights, owner(0, -1, 1, -2, 2, -3, 3, 4), None, BF16)


def solution(mesh):
    in_specs = (
        P("fsdp", None),
        P("fsdp", "ctx"),
        P("ctx", "fsdp"),
        P(("fsdp", "ctx"), None),
        P(("fsdp", "ctx"), None),
        P("fsdp", None, None),
    )
    return jax.shard_map(body, mesh=mesh, in_specs=in_specs, out_specs=P("fsdp", "ctx"), check_vma=False)
```

```python
import functools

import jax
import jax.numpy as jnp
from jax import lax
from jax.experimental import pallas as pl
from jax.experimental.pallas import tpu as pltpu
from jax.sharding import PartitionSpec as P

HEAD = 128
BLOCK = 128
SIDE = 4
ROPE_BASE = 1000000.0
F32 = jnp.float32
BF16 = jnp.bfloat16
VMEM_LIMIT = 48 * 2**20


def fsdp_index(y, x, core):
    return ((y % SIDE) * SIDE + x % SIDE) * 2 + core


def ring_pairs(phase, step):
    pairs = []
    for y in range(SIDE):
        for x in range(SIDE):
            for core in range(2):
                along_x = (core == 0) == (phase == 0)
                target = (y, x + step) if along_x else (y + step, x)
                pairs.append((fsdp_index(y, x, core), fsdp_index(*target, core)))
    return pairs


CORE_PAIRS = [(f, f ^ 1) for f in range(2 * SIDE * SIDE)]


def swap_cores(block):
    return lax.ppermute(block, "fsdp", CORE_PAIRS)


FIRST = (0, -1, 1, 2)


def block_index(core, first, second):
    me = lax.axis_index("fsdp") // 2
    y, x = me // SIDE, me % SIDE
    dx = jnp.where(core == 0, first, second)
    dy = jnp.where(core == 0, second, first)
    return (((y + dy) % SIDE) * SIDE + (x + dx) % SIDE) * 2 + core


def project_kernel(terms, has_sum, index_ref, *refs):
    tokens, weights = refs[:terms], refs[terms : 2 * terms]
    rest = refs[2 * terms :]
    before = rest[0] if has_sum else None
    out, total = rest[-2], rest[-1]
    step = pl.program_id(0)

    @pl.when(step == 0)
    def _():
        if has_sum:
            total[...] = before[...]
        else:
            total[...] = jnp.zeros_like(total)

    added = jnp.dot(tokens[0][...], weights[0][...], preferred_element_type=F32)
    for t, w in zip(tokens[1:], weights[1:]):
        added += jnp.dot(t[...], w[...], preferred_element_type=F32)
    total[...] += added

    @pl.when(step == pl.num_programs(0) - 1)
    def _():
        out[...] = total[...]


def project(tokens, pieces, index, before=None, vmem=VMEM_LIMIT):
    rows = tokens.shape[0]
    terms = len(pieces)
    depth, cols = tokens.shape[1] // (2 * SIDE * SIDE), pieces[0].shape[1]
    steps = pieces[0].shape[0] // depth

    def token_spec(t):
        return pl.BlockSpec((rows, depth), lambda i, index_ref: (0, index_ref[t, i]))

    whole = pl.BlockSpec((rows, cols), lambda i, index_ref: (0, 0))
    piece_spec = pl.BlockSpec((depth, cols), lambda i, index_ref: (i, 0))
    sums = [] if before is None else [before]
    return pl.pallas_call(
        functools.partial(project_kernel, terms, before is not None),
        grid_spec=pltpu.PrefetchScalarGridSpec(
            num_scalar_prefetch=1,
            grid=(steps,),
            in_specs=[token_spec(t) for t in range(terms)] + [piece_spec] * terms + [whole] * len(sums),
            out_specs=whole,
            scratch_shapes=[pltpu.VMEM((rows, cols), F32)],
        ),
        out_shape=jax.ShapeDtypeStruct((rows, cols), F32),
        compiler_params=pltpu.CompilerParams(vmem_limit_bytes=vmem),
        cost_estimate=pl.CostEstimate(
            flops=2 * rows * cols * depth * steps * terms,
            bytes_accessed=2 * (rows + cols) * depth * steps * terms + 8 * rows * cols,
            transcendentals=0,
        ),
        name="project",
    )(index, *([tokens] * terms), *pieces, *sums)


def attend_kernel(heads, entries, first, own_first, blocks_ref, q_ref, cos_ref, sin_ref, kv_ref, out_ref, keys, values, queries):
    b = first + pl.program_id(0)
    own = own_first + b
    for n in range(entries):
        block = blocks_ref[b, n]
        row = pl.multiple_of((block % 2) * BLOCK, BLOCK)
        keys[pl.ds(n * BLOCK, BLOCK), :] = kv_ref[block // 2, 0, pl.ds(row, BLOCK), :]
        values[pl.ds(n * BLOCK, BLOCK), :] = kv_ref[block // 2, 1, pl.ds(row, BLOCK), :]
    query_row = lax.broadcasted_iota(jnp.int32, (BLOCK, BLOCK), 0)
    key_row = lax.broadcasted_iota(jnp.int32, (BLOCK, BLOCK), 1)
    late = key_row > query_row
    cos, sin = cos_ref[...], sin_ref[...]
    for h in range(heads):
        x = q_ref[:, h * HEAD : (h + 1) * HEAD]
        queries[h * BLOCK : (h + 1) * BLOCK, :] = (x * cos + pltpu.roll(x, HEAD // 2, 1) * sin).astype(BF16)
    scores = lax.dot_general(queries[...], keys[...], (((1,), (1,)), ((), ())), preferred_element_type=F32)
    hidden = [jnp.logical_and(late, blocks_ref[b, n] == own) for n in range(entries)]
    for h in range(heads):
        strip = scores[h * BLOCK : (h + 1) * BLOCK, :]
        kept = [jnp.where(hidden[n], -jnp.inf, strip[:, n * BLOCK : (n + 1) * BLOCK]) for n in range(entries)]
        strip = jnp.concatenate(kept, axis=1)
        raised = jnp.exp(strip - jnp.max(strip, axis=1, keepdims=True))
        total = jnp.sum(raised, axis=1, keepdims=True)
        mixed = jnp.dot(raised.astype(BF16), values[...], preferred_element_type=F32)
        out_ref[:, h * HEAD : (h + 1) * HEAD] = (mixed / total).astype(BF16)


def attend(projected, cos, sin, kv, lists, first, count):
    cols = projected.shape[1]
    query_blocks, entries = lists.shape
    owners, _, held, _ = kv.shape
    heads = cols // HEAD
    rows = count * BLOCK
    own_first = owners * held // BLOCK - query_blocks
    table = pl.BlockSpec((BLOCK, HEAD), lambda b, lists_ref: (first + b, 0))
    return pl.pallas_call(
        functools.partial(attend_kernel, heads, entries, first, own_first),
        grid_spec=pltpu.PrefetchScalarGridSpec(
            num_scalar_prefetch=1,
            grid=(count,),
            in_specs=[
                pl.BlockSpec((BLOCK, cols), lambda b, lists_ref: (first + b, 0)),
                table,
                table,
                pl.BlockSpec(kv.shape, lambda b, lists_ref: (0, 0, 0, 0)),
            ],
            out_specs=pl.BlockSpec((BLOCK, cols), lambda b, lists_ref: (b, 0)),
            scratch_shapes=[
                pltpu.VMEM((entries * BLOCK, HEAD), BF16),
                pltpu.VMEM((entries * BLOCK, HEAD), BF16),
                pltpu.VMEM((heads * BLOCK, HEAD), BF16),
            ],
        ),
        out_shape=jax.ShapeDtypeStruct((rows, cols), BF16),
        compiler_params=pltpu.CompilerParams(vmem_limit_bytes=VMEM_LIMIT),
        cost_estimate=pl.CostEstimate(
            flops=4 * rows * entries * BLOCK * cols,
            bytes_accessed=6 * rows * cols + 2 * kv.size,
            transcendentals=rows * heads * entries * BLOCK,
        ),
        name="attend",
    )(lists, projected, cos, sin, kv)


def output_kernel(terms, has_sum, index_ref, *refs):
    contexts, weights = refs[: 2 * terms], refs[2 * terms : 3 * terms]
    out = refs[-1]
    rows = contexts[0].shape[0]
    for half in range(2):
        here = pl.ds(half * rows, rows)
        total = jnp.dot(contexts[half][...], weights[0][0], preferred_element_type=F32)
        for t in range(1, terms):
            total += jnp.dot(contexts[2 * t + half][...], weights[t][0], preferred_element_type=F32)
        if has_sum:
            total += refs[3 * terms][here, :]
        out[here, :] = total.astype(out.dtype)


def output(contexts, weights, index, before=None, dtype=F32):
    rows, depth = contexts[0][0].shape
    terms = len(contexts)
    width = weights.shape[2]
    parts = index.shape[1]

    def weight_spec(t):
        return pl.BlockSpec((1, depth, width), lambda j, index_ref: (index_ref[t, j], 0, 0))

    strip = pl.BlockSpec((2 * rows, width), lambda j, index_ref: (0, j))
    sums = [] if before is None else [before]
    return pl.pallas_call(
        functools.partial(output_kernel, terms, before is not None),
        grid_spec=pltpu.PrefetchScalarGridSpec(
            num_scalar_prefetch=1,
            grid=(parts,),
            in_specs=[pl.BlockSpec((rows, depth), lambda j, index_ref: (0, 0))] * (2 * terms)
            + [weight_spec(t) for t in range(terms)]
            + [strip] * len(sums),
            out_specs=strip,
        ),
        out_shape=jax.ShapeDtypeStruct((2 * rows, parts * width), dtype),
        compiler_params=pltpu.CompilerParams(vmem_limit_bytes=VMEM_LIMIT),
        cost_estimate=pl.CostEstimate(
            flops=4 * rows * depth * width * parts * terms,
            bytes_accessed=2 * depth * (2 * rows + width * parts) * terms + 16 * rows * width * parts,
            transcendentals=0,
        ),
        name="output",
    )(index, *[c for pair in contexts for c in pair], *([weights] * terms), *sums)


def tables(rows, first):
    frequency = ROPE_BASE ** (-(jnp.arange(HEAD // 2, dtype=F32) * 2.0) / HEAD)
    positions = (first + jnp.arange(rows, dtype=jnp.int32)).astype(F32)
    angles = positions[:, None] * frequency[None, :]
    scale = HEAD ** (-0.5)
    cos, sin = jnp.cos(angles) * scale, jnp.sin(angles) * scale
    return jnp.concatenate([cos, cos], axis=1), jnp.concatenate([-sin, sin], axis=1)


def side_by_side_kernel(count, *refs):
    pieces, out, done = refs[:count], refs[count], refs[count + 1]
    copies = []
    start = 0
    for n, piece in enumerate(pieces):
        size = piece.shape[0]
        copies.append(pltpu.make_async_copy(piece, out.at[pl.ds(start, size)], done.at[n]))
        start += size
    for copy in copies:
        copy.start()
    for copy in copies:
        copy.wait()


def side_by_side(pieces):
    total = sum(p.shape[0] for p in pieces)
    anywhere = pl.BlockSpec(memory_space=pl.ANY)
    out = jax.ShapeDtypeStruct((total,) + pieces[0].shape[1:], pieces[0].dtype)
    return pl.pallas_call(
        functools.partial(side_by_side_kernel, len(pieces)),
        in_specs=[anywhere] * len(pieces),
        out_specs=anywhere,
        out_shape=out,
        scratch_shapes=[pltpu.SemaphoreType.DMA((len(pieces),))],
        compiler_params=pltpu.CompilerParams(vmem_limit_bytes=VMEM_LIMIT),
        cost_estimate=pl.CostEstimate(flops=0, bytes_accessed=4 * out.size, transcendentals=0),
        name="side_by_side",
    )(*pieces)


def split_heads_kernel(keys, values, out):
    out[0, 0] = keys[...]
    out[0, 1] = values[...]


def split_heads(keys, values):
    held, cols = keys.shape
    heads = cols // HEAD
    column = pl.BlockSpec((held, HEAD), lambda h: (0, h))
    return pl.pallas_call(
        split_heads_kernel,
        grid=(heads,),
        in_specs=[column, column],
        out_specs=pl.BlockSpec((1, 2, held, HEAD), lambda h: (h, 0, 0, 0)),
        out_shape=jax.ShapeDtypeStruct((heads, 2, held, HEAD), keys.dtype),
        compiler_params=pltpu.CompilerParams(vmem_limit_bytes=VMEM_LIMIT),
        cost_estimate=pl.CostEstimate(flops=0, bytes_accessed=8 * keys.size, transcendentals=0),
        name="split_heads",
    )(keys, values)


def after(value, *earlier):
    return lax.optimization_barrier((value,) + earlier)[0]


def wo_target(f, c):
    core, x, y = f % 2, f // 2 % SIDE, f // 2 // SIDE
    x_to = jnp.where(c % 2 == 0, x, x + jnp.where(x % 2 == 0, -1, 1))
    return fsdp_index(y + c // 2, x_to, core)


def wo_moves(fsdp_count, ctx_count):
    parts = fsdp_count // ctx_count
    within, across = [], []
    for f in range(fsdp_count):
        for c in range(ctx_count):
            core, x, y = f % 2, f // 2 % SIDE, f // 2 // SIDE
            x_to = x if c % 2 == 0 else x + (-1 if x % 2 == 0 else 1)
            target = fsdp_index(y + c // 2, x_to, core) * ctx_count
            within.append((f * ctx_count + c, target + c))
            across.append((target + c, target + f // parts))
    return within, across


def project_all(tokens, wq, by_head, wo_near, wo_across, turns):
    own_line, near, far_away = wq_indices()
    minus = lax.ppermute(wq, "fsdp", ring_pairs(0, 1))
    plus = lax.ppermute(wq, "fsdp", ring_pairs(0, -1))
    far = lax.ppermute(wq, "fsdp", ring_pairs(0, 2))
    far, _, wo_near, turns = lax.optimization_barrier((far, by_head, wo_near, turns))
    line = side_by_side([wq, minus, plus, far])
    wo_here = lax.ppermute(wo_near, ("fsdp", "ctx"), wo_across)
    kv = lax.all_to_all(after(by_head, wo_here), "ctx", 0, 0, tiled=True)
    half = line.shape[0] // 2
    line_minus = lax.ppermute(line, "fsdp", ring_pairs(1, 1))
    line_plus = lax.ppermute(line, "fsdp", ring_pairs(1, -1))
    first = project(tokens, [line, swap_cores(line)], own_line)
    top, low, waited = lax.optimization_barrier((line_minus[:half], line_plus[half:], first))
    far_top = lax.ppermute(top, "fsdp", ring_pairs(1, 1))
    far_low = lax.ppermute(low, "fsdp", ring_pairs(1, -1))
    second = project(
        tokens, [line_minus, line_plus, swap_cores(line_minus), swap_cores(line_plus)], near, waited
    )
    far_top, far_low, second = lax.optimization_barrier((far_top, far_low, second))
    third = project(tokens, [far_top, far_low, swap_cores(far_top), swap_cores(far_low)], far_away, second, 60 * 2**20)
    return third, turns, kv, after(wo_here, first, line_minus, line_plus)


def wq_indices():
    core = lax.axis_index("fsdp") % 2
    cores = (core, 1 - core)

    def rows(which, second, firsts):
        return jnp.stack([block_index(which, o, second) for o in firsts])

    return [
        jnp.stack([rows(k, 0, FIRST) for k in cores]),
        jnp.stack([rows(k, s, FIRST) for k in cores for s in (-1, 1)]),
        jnp.stack([rows(k, 2, part) for k in cores for part in (FIRST[:2], FIRST[2:])]),
    ]


def body(tokens, wq, wo, key_cache, value_cache, key_blocks):
    ctx_count = lax.axis_size("ctx")
    fsdp_count = lax.axis_size("fsdp")
    z = lax.axis_index("ctx")
    rows = tokens.shape[0]
    held = key_cache.shape[0]

    parts = fsdp_count // ctx_count
    within, across = wo_moves(fsdp_count, ctx_count)
    wo_near = lax.ppermute(wo, ("fsdp", "ctx"), within)
    by_head = split_heads(key_cache, value_cache)
    turns = tables(rows, held * ctx_count - rows)
    projected, (cos, sin), kv, wo_here = project_all(tokens, wq, by_head, wo_near, across, turns)
    weights = lax.all_gather(wo_here, "fsdp", axis=0, tiled=False)

    blocks = rows // BLOCK // 2
    contexts = [attend(projected, cos, sin, kv, key_blocks[0], n * blocks, blocks) for n in range(2)]

    def owner(*offsets):
        def at(offset):
            return jnp.stack([wo_target(z * parts + j, (z + offset) % ctx_count) for j in range(parts)])

        return jnp.stack([at(o) for o in offsets])

    right = [(i, (i + 1) % ctx_count) for i in range(ctx_count)]
    left = [(i, (i - 1) % ctx_count) for i in range(ctx_count)]
    down, up = [contexts], [contexts]
    for _ in range(3):
        down.append([lax.ppermute(c, "ctx", right) for c in down[-1]])
        up.append([lax.ppermute(c, "ctx", left) for c in up[-1]])
    weights, last_down, last_up = lax.optimization_barrier((weights, down[3][0], up[3][1]))
    far = [lax.ppermute(last_down, "ctx", right), lax.ppermute(last_up, "ctx", left)]
    total = output([contexts, down[1], up[1], down[2], up[2]], weights, owner(0, -1, 1, -2, 2))
    return output([down[3], up[3], far], weights, owner(-3, 3, 4), total, BF16)


def solution(mesh):
    in_specs = (
        P("fsdp", None),
        P("fsdp", "ctx"),
        P("ctx", "fsdp"),
        P(("fsdp", "ctx"), None),
        P(("fsdp", "ctx"), None),
        P("fsdp", None, None),
    )
    return jax.shard_map(body, mesh=mesh, in_specs=in_specs, out_specs=P("fsdp", "ctx"), check_vma=False)
```

```python
import functools

import jax
import jax.numpy as jnp
from jax import lax
from jax.experimental import pallas as pl
from jax.experimental.pallas import tpu as pltpu
from jax.sharding import PartitionSpec as P

HEAD = 128
BLOCK = 128
SIDE = 4
ROPE_BASE = 1000000.0
F32 = jnp.float32
BF16 = jnp.bfloat16
VMEM_LIMIT = 48 * 2**20


def fsdp_index(y, x, core):
    return ((y % SIDE) * SIDE + x % SIDE) * 2 + core


def ring_pairs(phase, step):
    pairs = []
    for y in range(SIDE):
        for x in range(SIDE):
            for core in range(2):
                along_x = (core == 0) == (phase == 0)
                target = (y, x + step) if along_x else (y + step, x)
                pairs.append((fsdp_index(y, x, core), fsdp_index(*target, core)))
    return pairs


CORE_PAIRS = [(f, f ^ 1) for f in range(2 * SIDE * SIDE)]


def swap_cores(block):
    return lax.ppermute(block, "fsdp", CORE_PAIRS)


FIRST = (0, -1, 1, 2)


def block_index(core, first, second):
    me = lax.axis_index("fsdp") // 2
    y, x = me // SIDE, me % SIDE
    dx = jnp.where(core == 0, first, second)
    dy = jnp.where(core == 0, second, first)
    return (((y + dy) % SIDE) * SIDE + (x + dx) % SIDE) * 2 + core


def project_kernel(terms, has_sum, index_ref, *refs):
    tokens, weights = refs[:terms], refs[terms : 2 * terms]
    rest = refs[2 * terms :]
    before = rest[0] if has_sum else None
    out, total = rest[-2], rest[-1]
    step = pl.program_id(0)

    @pl.when(step == 0)
    def _():
        if has_sum:
            total[...] = before[...]
        else:
            total[...] = jnp.zeros_like(total)

    added = jnp.dot(tokens[0][...], weights[0][...], preferred_element_type=F32)
    for t, w in zip(tokens[1:], weights[1:]):
        added += jnp.dot(t[...], w[...], preferred_element_type=F32)
    total[...] += added

    @pl.when(step == pl.num_programs(0) - 1)
    def _():
        out[...] = total[...]


def project(tokens, pieces, index, before=None, vmem=VMEM_LIMIT):
    rows = tokens.shape[0]
    terms = len(pieces)
    depth, cols = tokens.shape[1] // (2 * SIDE * SIDE), pieces[0].shape[1]
    steps = pieces[0].shape[0] // depth

    def token_spec(t):
        return pl.BlockSpec((rows, depth), lambda i, index_ref: (0, index_ref[t, i]))

    whole = pl.BlockSpec((rows, cols), lambda i, index_ref: (0, 0))
    piece_spec = pl.BlockSpec((depth, cols), lambda i, index_ref: (i, 0))
    sums = [] if before is None else [before]
    return pl.pallas_call(
        functools.partial(project_kernel, terms, before is not None),
        grid_spec=pltpu.PrefetchScalarGridSpec(
            num_scalar_prefetch=1,
            grid=(steps,),
            in_specs=[token_spec(t) for t in range(terms)] + [piece_spec] * terms + [whole] * len(sums),
            out_specs=whole,
            scratch_shapes=[pltpu.VMEM((rows, cols), F32)],
        ),
        out_shape=jax.ShapeDtypeStruct((rows, cols), F32),
        compiler_params=pltpu.CompilerParams(vmem_limit_bytes=vmem),
        cost_estimate=pl.CostEstimate(
            flops=2 * rows * cols * depth * steps * terms,
            bytes_accessed=2 * (rows + cols) * depth * steps * terms + 8 * rows * cols,
            transcendentals=0,
        ),
        name="project",
    )(index, *([tokens] * terms), *pieces, *sums)


def attend_kernel(heads, entries, first, own_first, blocks_ref, q_ref, cos_ref, sin_ref, kv_ref, out_ref, keys, values, queries):
    b = first + pl.program_id(0)
    own = own_first + b
    for n in range(entries):
        block = blocks_ref[b, n]
        row = pl.multiple_of((block % 2) * BLOCK, BLOCK)
        keys[pl.ds(n * BLOCK, BLOCK), :] = kv_ref[block // 2, 0, pl.ds(row, BLOCK), :]
        values[pl.ds(n * BLOCK, BLOCK), :] = kv_ref[block // 2, 1, pl.ds(row, BLOCK), :]
    query_row = lax.broadcasted_iota(jnp.int32, (BLOCK, BLOCK), 0)
    key_row = lax.broadcasted_iota(jnp.int32, (BLOCK, BLOCK), 1)
    late = key_row > query_row
    cos, sin = cos_ref[...], sin_ref[...]
    for h in range(heads):
        x = q_ref[:, h * HEAD : (h + 1) * HEAD]
        queries[h * BLOCK : (h + 1) * BLOCK, :] = (x * cos + pltpu.roll(x, HEAD // 2, 1) * sin).astype(BF16)
    scores = lax.dot_general(queries[...], keys[...], (((1,), (1,)), ((), ())), preferred_element_type=F32)
    hidden = [jnp.logical_and(late, blocks_ref[b, n] == own) for n in range(entries)]
    for h in range(heads):
        strip = scores[h * BLOCK : (h + 1) * BLOCK, :]
        kept = [jnp.where(hidden[n], -jnp.inf, strip[:, n * BLOCK : (n + 1) * BLOCK]) for n in range(entries)]
        strip = jnp.concatenate(kept, axis=1)
        raised = jnp.exp(strip - jnp.max(strip, axis=1, keepdims=True))
        total = jnp.sum(raised, axis=1, keepdims=True)
        mixed = jnp.dot(raised.astype(BF16), values[...], preferred_element_type=F32)
        out_ref[:, h * HEAD : (h + 1) * HEAD] = (mixed / total).astype(BF16)


def attend(projected, cos, sin, kv, lists, first, count):
    cols = projected.shape[1]
    query_blocks, entries = lists.shape
    owners, _, held, _ = kv.shape
    heads = cols // HEAD
    rows = count * BLOCK
    own_first = owners * held // BLOCK - query_blocks
    table = pl.BlockSpec((BLOCK, HEAD), lambda b, lists_ref: (first + b, 0))
    return pl.pallas_call(
        functools.partial(attend_kernel, heads, entries, first, own_first),
        grid_spec=pltpu.PrefetchScalarGridSpec(
            num_scalar_prefetch=1,
            grid=(count,),
            in_specs=[
                pl.BlockSpec((BLOCK, cols), lambda b, lists_ref: (first + b, 0)),
                table,
                table,
                pl.BlockSpec(kv.shape, lambda b, lists_ref: (0, 0, 0, 0)),
            ],
            out_specs=pl.BlockSpec((BLOCK, cols), lambda b, lists_ref: (b, 0)),
            scratch_shapes=[
                pltpu.VMEM((entries * BLOCK, HEAD), BF16),
                pltpu.VMEM((entries * BLOCK, HEAD), BF16),
                pltpu.VMEM((heads * BLOCK, HEAD), BF16),
            ],
        ),
        out_shape=jax.ShapeDtypeStruct((rows, cols), BF16),
        compiler_params=pltpu.CompilerParams(vmem_limit_bytes=VMEM_LIMIT),
        cost_estimate=pl.CostEstimate(
            flops=4 * rows * entries * BLOCK * cols,
            bytes_accessed=6 * rows * cols + 2 * kv.size,
            transcendentals=rows * heads * entries * BLOCK,
        ),
        name="attend",
    )(lists, projected, cos, sin, kv)


def output_kernel(terms, has_sum, index_ref, *refs):
    contexts, weights = refs[: 2 * terms], refs[2 * terms : 3 * terms]
    out = refs[-1]
    rows = contexts[0].shape[0]
    for half in range(2):
        here = pl.ds(half * rows, rows)
        total = jnp.dot(contexts[half][...], weights[0][0], preferred_element_type=F32)
        for t in range(1, terms):
            total += jnp.dot(contexts[2 * t + half][...], weights[t][0], preferred_element_type=F32)
        if has_sum:
            total += refs[3 * terms][here, :]
        out[here, :] = total.astype(out.dtype)


def output(contexts, weights, index, before=None, dtype=F32):
    rows, depth = contexts[0][0].shape
    terms = len(contexts)
    width = weights.shape[2]
    parts = index.shape[1]

    def weight_spec(t):
        return pl.BlockSpec((1, depth, width), lambda j, index_ref: (index_ref[t, j], 0, 0))

    strip = pl.BlockSpec((2 * rows, width), lambda j, index_ref: (0, j))
    sums = [] if before is None else [before]
    return pl.pallas_call(
        functools.partial(output_kernel, terms, before is not None),
        grid_spec=pltpu.PrefetchScalarGridSpec(
            num_scalar_prefetch=1,
            grid=(parts,),
            in_specs=[pl.BlockSpec((rows, depth), lambda j, index_ref: (0, 0))] * (2 * terms)
            + [weight_spec(t) for t in range(terms)]
            + [strip] * len(sums),
            out_specs=strip,
        ),
        out_shape=jax.ShapeDtypeStruct((2 * rows, parts * width), dtype),
        compiler_params=pltpu.CompilerParams(vmem_limit_bytes=VMEM_LIMIT),
        cost_estimate=pl.CostEstimate(
            flops=4 * rows * depth * width * parts * terms,
            bytes_accessed=2 * depth * (2 * rows + width * parts) * terms + 16 * rows * width * parts,
            transcendentals=0,
        ),
        name="output",
    )(index, *[c for pair in contexts for c in pair], *([weights] * terms), *sums)


def tables(rows, first):
    frequency = ROPE_BASE ** (-(jnp.arange(HEAD // 2, dtype=F32) * 2.0) / HEAD)
    positions = (first + jnp.arange(rows, dtype=jnp.int32)).astype(F32)
    angles = positions[:, None] * frequency[None, :]
    scale = HEAD ** (-0.5)
    cos, sin = jnp.cos(angles) * scale, jnp.sin(angles) * scale
    return jnp.concatenate([cos, cos], axis=1), jnp.concatenate([-sin, sin], axis=1)


def side_by_side_kernel(count, *refs):
    pieces, out, done = refs[:count], refs[count], refs[count + 1]
    copies = []
    start = 0
    for n, piece in enumerate(pieces):
        size = piece.shape[0]
        copies.append(pltpu.make_async_copy(piece, out.at[pl.ds(start, size)], done.at[n]))
        start += size
    for copy in copies:
        copy.start()
    for copy in copies:
        copy.wait()


def side_by_side(pieces):
    total = sum(p.shape[0] for p in pieces)
    anywhere = pl.BlockSpec(memory_space=pl.ANY)
    out = jax.ShapeDtypeStruct((total,) + pieces[0].shape[1:], pieces[0].dtype)
    return pl.pallas_call(
        functools.partial(side_by_side_kernel, len(pieces)),
        in_specs=[anywhere] * len(pieces),
        out_specs=anywhere,
        out_shape=out,
        scratch_shapes=[pltpu.SemaphoreType.DMA((len(pieces),))],
        compiler_params=pltpu.CompilerParams(vmem_limit_bytes=VMEM_LIMIT),
        cost_estimate=pl.CostEstimate(flops=0, bytes_accessed=4 * out.size, transcendentals=0),
        name="side_by_side",
    )(*pieces)


def split_heads_kernel(keys, values, out):
    out[0, 0] = keys[...]
    out[0, 1] = values[...]


def split_heads(keys, values):
    held, cols = keys.shape
    heads = cols // HEAD
    column = pl.BlockSpec((held, HEAD), lambda h: (0, h))
    return pl.pallas_call(
        split_heads_kernel,
        grid=(heads,),
        in_specs=[column, column],
        out_specs=pl.BlockSpec((1, 2, held, HEAD), lambda h: (h, 0, 0, 0)),
        out_shape=jax.ShapeDtypeStruct((heads, 2, held, HEAD), keys.dtype),
        compiler_params=pltpu.CompilerParams(vmem_limit_bytes=VMEM_LIMIT),
        cost_estimate=pl.CostEstimate(flops=0, bytes_accessed=8 * keys.size, transcendentals=0),
        name="split_heads",
    )(keys, values)


def after(value, *earlier):
    return lax.optimization_barrier((value,) + earlier)[0]


def wo_target(f, c):
    core, x, y = f % 2, f // 2 % SIDE, f // 2 // SIDE
    x_to = jnp.where(c % 2 == 0, x, x + jnp.where(x % 2 == 0, -1, 1))
    return fsdp_index(y + c // 2, x_to, core)


def wo_moves(fsdp_count, ctx_count):
    parts = fsdp_count // ctx_count
    within, across = [], []
    for f in range(fsdp_count):
        for c in range(ctx_count):
            core, x, y = f % 2, f // 2 % SIDE, f // 2 // SIDE
            x_to = x if c % 2 == 0 else x + (-1 if x % 2 == 0 else 1)
            target = fsdp_index(y + c // 2, x_to, core) * ctx_count
            within.append((f * ctx_count + c, target + c))
            across.append((target + c, target + f // parts))
    return within, across


def project_all(tokens, wq, by_head, wo_near, wo_across, turns):
    own_line, near, far_away = wq_indices()
    minus = lax.ppermute(wq, "fsdp", ring_pairs(0, 1))
    plus = lax.ppermute(wq, "fsdp", ring_pairs(0, -1))
    far = lax.ppermute(wq, "fsdp", ring_pairs(0, 2))
    far, _, wo_near, turns = lax.optimization_barrier((far, by_head, wo_near, turns))
    line = side_by_side([wq, minus, plus, far])
    wo_here = lax.ppermute(wo_near, ("fsdp", "ctx"), wo_across)
    kv = lax.all_to_all(after(by_head, wo_here), "ctx", 0, 0, tiled=True)
    half = line.shape[0] // 2
    line_minus = lax.ppermute(line, "fsdp", ring_pairs(1, 1))
    line_plus = lax.ppermute(line, "fsdp", ring_pairs(1, -1))
    first = project(tokens, [line, swap_cores(line)], own_line)
    top, low, waited = lax.optimization_barrier((line_minus[:half], line_plus[half:], first))
    far_top = lax.ppermute(top, "fsdp", ring_pairs(1, 1))
    far_low = lax.ppermute(low, "fsdp", ring_pairs(1, -1))
    second = project(
        tokens, [line_minus, line_plus, swap_cores(line_minus), swap_cores(line_plus)], near, waited
    )
    far_top, far_low, second = lax.optimization_barrier((far_top, far_low, second))
    third = project(tokens, [far_top, far_low, swap_cores(far_top), swap_cores(far_low)], far_away, second, 60 * 2**20)
    return third, turns, kv, after(wo_here, first, line_minus, line_plus)


def wq_indices():
    core = lax.axis_index("fsdp") % 2
    cores = (core, 1 - core)

    def rows(which, second, firsts):
        return jnp.stack([block_index(which, o, second) for o in firsts])

    return [
        jnp.stack([rows(k, 0, FIRST) for k in cores]),
        jnp.stack([rows(k, s, FIRST) for k in cores for s in (-1, 1)]),
        jnp.stack([rows(k, 2, part) for k in cores for part in (FIRST[:2], FIRST[2:])]),
    ]


def body(tokens, wq, wo, key_cache, value_cache, key_blocks):
    ctx_count = lax.axis_size("ctx")
    fsdp_count = lax.axis_size("fsdp")
    z = lax.axis_index("ctx")
    rows = tokens.shape[0]
    held = key_cache.shape[0]

    parts = fsdp_count // ctx_count
    within, across = wo_moves(fsdp_count, ctx_count)
    wo_near = lax.ppermute(wo, ("fsdp", "ctx"), within)
    by_head = split_heads(key_cache, value_cache)
    turns = tables(rows, held * ctx_count - rows)
    projected, (cos, sin), kv, wo_here = project_all(tokens, wq, by_head, wo_near, across, turns)
    weights = lax.all_gather(wo_here, "fsdp", axis=0, tiled=False)

    blocks = rows // BLOCK // 2
    contexts = [attend(projected, cos, sin, kv, key_blocks[0], n * blocks, blocks) for n in range(2)]

    def owner(*offsets):
        def at(offset):
            return jnp.stack([wo_target(z * parts + j, (z + offset) % ctx_count) for j in range(parts)])

        return jnp.stack([at(o) for o in offsets])

    right = [(i, (i + 1) % ctx_count) for i in range(ctx_count)]
    left = [(i, (i - 1) % ctx_count) for i in range(ctx_count)]
    down, up = [contexts], [contexts]
    for _ in range(3):
        down.append([lax.ppermute(c, "ctx", right) for c in down[-1]])
        up.append([lax.ppermute(c, "ctx", left) for c in up[-1]])
    weights, last_down, last_up = lax.optimization_barrier((weights, down[3][0], up[3][1]))
    far = [lax.ppermute(last_down, "ctx", right), lax.ppermute(last_up, "ctx", left)]
    total = output([contexts, down[1], up[1], down[2], up[2], down[3]], weights, owner(0, -1, 1, -2, 2, -3))
    return output([up[3], far], weights, owner(3, 4), total, BF16)


def solution(mesh):
    in_specs = (
        P("fsdp", None),
        P("fsdp", "ctx"),
        P("ctx", "fsdp"),
        P(("fsdp", "ctx"), None),
        P(("fsdp", "ctx"), None),
        P("fsdp", None, None),
    )
    return jax.shard_map(body, mesh=mesh, in_specs=in_specs, out_specs=P("fsdp", "ctx"), check_vma=False)
```
